256 devices in a mesh: outer: 8 (over y, x_lo), inner: 32 (over z, x_hi, core).
Axes of the slice: x: 4 (x_hi: 2, x_lo: 2; x = x_hi * 2 + x_lo), y: 4, z: 8, core: 2. Of those that a mesh axis runs over, the one named last changes fastest.
Arguments:
- queries: bfloat16 [65536, 4096], P(('outer', 'inner')), may hold values from -6 to 6
- keys: bfloat16 [65536, 1024], P(('outer', 'inner')), may hold values from -6 to 6
- values: bfloat16 [65536, 1024], P(('outer', 'inner')), may hold values from -6 to 6
- grad_out: bfloat16 [65536, 4096], P(('outer', 'inner')), may hold values from -24 to 24
- log_sum: float32 [32, 65536], P(None, ('outer', 'inner')), as said below
- row_delta: float32 [32, 65536], P(None, ('outer', 'inner')), may hold values from -24 to 24
- piece_index: int32 [512], P(('outer', 'inner')), may hold values from 0 to 511, as said below
Outputs:
- grad_queries: bfloat16 [65536, 4096], P(('outer', 'inner'))
- grad_keys: float32 [65536, 1024], P(('outer', 'inner'))
- grad_values: float32 [65536, 1024], P(('outer', 'inner'))
The draws below stay inside these ranges and needn't reach their ends.
Inputs may be any that keep to these rules, and one draw needn't show every extreme that they name: `piece_index`: block b holds pieces p and 511 - p, the smaller first, where p runs over a permutation of 0 to 255 drawn from the seed; every piece appears once. `log_sum`: every entry lies within 1.5 of log(512).
All inputs are finite; a program needn't handle non-finite values.
Results may differ from the reference program's by a relative error of at most 0.0075.
Values may be sent and summed in bfloat16 or wider, within the bound.
A program may use at most 192 MiB of HBM per device.

```python
import math
import jax
import jax.numpy as jnp
from jax import lax

HEADS = 32
KV_HEADS = 8
HEAD_DIM = 128
TOK_DEV = 256
TOKENS = 65536
PIECES = 512
N_OUTER = 8
N_INNER = 32


def draw_piece_index(key, part):
    key = jax.random.fold_in(key, 11)
    order = jax.random.permutation(key, PIECES // 2).astype(jnp.int32)
    paired = jnp.stack([order, PIECES - 1 - order], axis=1)
    return paired.reshape(-1).astype(jnp.int32)


def draw_log_sum(key, part):
    key = jax.random.fold_in(key, 23)
    center = jnp.log(jnp.float32(2 * TOK_DEV))
    offset = jax.random.uniform(key, (HEADS, TOKENS), jnp.float32, -1.0, 1.0)
    return (center + offset).astype(jnp.float32)


def shard_levels(stream_key, extent, cuts, smallest, largest):
    gain, own = 1.0, jax.random.fold_in(stream_key, 6)
    for position, parts in cuts:
        heights = jnp.exp(jax.random.uniform(jax.random.fold_in(own, position), (parts,), jnp.float32, smallest / len(cuts), largest / len(cuts)))
        gain = gain * jnp.repeat(heights, extent[position] // parts).reshape([-1 if axis == position else 1 for axis in range(len(extent))])
    return gain


def centred(stream_key, extent, scale, limit, cuts=(), held_as=jnp.bfloat16):
    level = shard_levels(stream_key, extent, cuts, -0.22, 0.18) if cuts else 1.0
    drawn = jax.random.normal(stream_key, extent, jnp.float32) * scale * level
    return jnp.minimum(jnp.maximum(drawn, -limit), limit).astype(held_as)


def setup_inputs(seed: int = 0) -> dict:
    streams_of = jax.random.split(jax.random.key(seed), 8)
    queries = centred(streams_of[0], (TOKENS, HEADS * HEAD_DIM), 1.0, 6.0, ((0, 256),))
    keys = centred(streams_of[1], (TOKENS, KV_HEADS * HEAD_DIM), 1.0, 6.0, ((0, 256),))
    values = centred(streams_of[2], (TOKENS, KV_HEADS * HEAD_DIM), 1.0, 6.0, ((0, 256),))
    grad_out = centred(streams_of[3], (TOKENS, HEADS * HEAD_DIM), 4.0, 24.0, ((0, 256),))
    log_sum = draw_log_sum(jax.random.fold_in(streams_of[7], 71), 0)
    row_delta = centred(streams_of[5], (HEADS, TOKENS), 4.0, 24.0, ((1, 256),), jnp.float32)
    piece_index = draw_piece_index(jax.random.fold_in(streams_of[7], 71), 0)
    return dict(queries=queries, keys=keys, values=values, grad_out=grad_out, log_sum=log_sum, row_delta=row_delta, piece_index=piece_index)


def spots(pieces, half):
    return (pieces[:, None] * half + jnp.arange(half, dtype=jnp.int32)[None, :]).reshape(-1)

def pair_terms(queries, grad_out, log_sum, row_delta, query_pos, keys, values, key_pos):
    rows = queries.shape[0]
    key_rows = keys.shape[0]
    group = HEADS // KV_HEADS
    scale = 1.0 / math.sqrt(HEAD_DIM)
    query_heads = queries.astype(jnp.float32).reshape(rows, KV_HEADS, group, HEAD_DIM)
    out_heads = grad_out.astype(jnp.float32).reshape(rows, KV_HEADS, group, HEAD_DIM)
    key_heads = keys.astype(jnp.float32).reshape(key_rows, KV_HEADS, HEAD_DIM)
    value_heads = values.astype(jnp.float32).reshape(key_rows, KV_HEADS, HEAD_DIM)
    scores = jnp.einsum('qhgd,khd->hgqk', query_heads, key_heads) * scale
    lse = log_sum.reshape(KV_HEADS, group, rows)[..., None]
    delta = row_delta.reshape(KV_HEADS, group, rows)[..., None]
    visible = key_pos[None, :] <= query_pos[:, None]
    probs = jnp.where(visible[None, None], jnp.exp(scores - lse), jnp.float32(0.0))
    dprobs = jnp.einsum('qhgd,khd->hgqk', out_heads, value_heads)
    dscore = probs * (dprobs - delta)
    probs_b = lax.optimization_barrier(probs.astype(jnp.bfloat16)).astype(jnp.float32)
    dscore_b = lax.optimization_barrier(dscore.astype(jnp.bfloat16)).astype(jnp.float32)
    grad_v = jnp.einsum('hgqk,qhgd->khd', probs_b, out_heads).reshape(key_rows, KV_HEADS * HEAD_DIM)
    grad_k = (jnp.einsum('hgqk,qhgd->khd', dscore_b, query_heads) * scale).reshape(key_rows, KV_HEADS * HEAD_DIM)
    grad_q = (jnp.einsum('hgqk,khd->qhgd', dscore_b, key_heads) * scale).reshape(rows, HEADS * HEAD_DIM)
    return (grad_q, grad_k, grad_v)

def reference(queries, keys, values, grad_out, log_sum, row_delta, piece_index):
    rows = TOK_DEV
    half = rows // 2
    blocks = N_OUTER * N_INNER

    def step(index, carry):
        grad_queries, grad_keys, grad_values = carry
        block = jnp.asarray(index).astype(jnp.int32)
        outer_pos = block // N_INNER
        inner_pos = block % N_INNER
        sources = [block, outer_pos * N_INNER + (inner_pos - 1) % N_INNER, outer_pos * N_INNER + (inner_pos - 2) % N_INNER, (outer_pos - 1) % N_OUTER * N_INNER + inner_pos]
        start = (block * rows).astype(jnp.int32)
        query_rows = lax.dynamic_slice_in_dim(queries, start, rows, 0)
        out_rows = lax.dynamic_slice_in_dim(grad_out, start, rows, 0)
        lse_rows = lax.dynamic_slice_in_dim(log_sum, start, rows, 1)
        delta_rows = lax.dynamic_slice_in_dim(row_delta, start, rows, 1)
        query_pos = spots(lax.dynamic_slice_in_dim(piece_index, (2 * block).astype(jnp.int32), 2, 0), half)
        total = jnp.zeros((rows, HEADS * HEAD_DIM), jnp.float32)
        for source in sources:
            key_start = (source * rows).astype(jnp.int32)
            key_rows = lax.dynamic_slice_in_dim(keys, key_start, rows, 0)
            value_rows = lax.dynamic_slice_in_dim(values, key_start, rows, 0)
            key_pos = spots(lax.dynamic_slice_in_dim(piece_index, (2 * source).astype(jnp.int32), 2, 0), half)
            grad_q, grad_k, grad_v = pair_terms(query_rows, out_rows, lse_rows, delta_rows, query_pos, key_rows, value_rows, key_pos)
            total = total + grad_q
            grad_keys = lax.dynamic_update_slice_in_dim(grad_keys, lax.dynamic_slice_in_dim(grad_keys, key_start, rows, 0) + grad_k, key_start, 0)
            grad_values = lax.dynamic_update_slice_in_dim(grad_values, lax.dynamic_slice_in_dim(grad_values, key_start, rows, 0) + grad_v, key_start, 0)
        grad_queries = lax.dynamic_update_slice_in_dim(grad_queries, total.astype(jnp.bfloat16), start, 0)
        return (grad_queries, grad_keys, grad_values)
    start_carry = (jnp.zeros((TOKENS, HEADS * HEAD_DIM), jnp.bfloat16), jnp.zeros((TOKENS, KV_HEADS * HEAD_DIM), jnp.float32), jnp.zeros((TOKENS, KV_HEADS * HEAD_DIM), jnp.float32))
    grad_queries, grad_keys, grad_values = lax.fori_loop(0, blocks, step, start_carry)
    return (grad_queries, grad_keys, grad_values)
```

```python
import functools
import math

import jax
import jax.numpy as jnp
from jax import lax
from jax.experimental import pallas as pl
from jax.experimental.pallas import tpu as pltpu
from jax.sharding import PartitionSpec as P

HEAD_DIM = 128
HALF = 128
MESH = pl.DeviceIdType.MESH
SCALE = 1.0 / math.sqrt(HEAD_DIM)
LOG2E = math.log2(math.e)
COMM = True
COMPUTE = True

BF16 = jnp.bfloat16
F32 = jnp.float32


def dot_nt(a, b):
    return lax.dot_general(a, b, (((1,), (1,)), ((), ())), preferred_element_type=F32)


def dot_nn(a, b):
    return lax.dot_general(a, b, (((1,), (0,)), ((), ())), preferred_element_type=F32)


def quadrant(k, v, q, do, lse2, delta, keep=None):
    p = jnp.exp2(dot_nt(k, q) * (SCALE * LOG2E) - lse2)
    if keep is not None:
        p = jnp.where(keep, p, 0.0)
    ds = p * (dot_nt(v, do) - delta)
    return p.astype(BF16), ds.astype(BF16)


def kernel(
    group,
    n_outer,
    n_inner,
    q_hbm,
    k_hbm,
    v_hbm,
    do_hbm,
    lse_hbm,
    delta_hbm,
    piece_ref,
    gq_hbm,
    gk_hbm,
    gv_hbm,
    q_v,
    do_v,
    lse_v,
    delta_v,
    lse_c,
    delta_c,
    kv_own,
    kv_grp,
    kv_far,
    kv_near,
    gq_acc,
    gq_out,
    own32,
    far32,
    grp32,
    n_send,
    n_recv,
    f_send,
    f_recv,
    s_send,
    s_recv,
    tile,
    flag,
    in_sem,
    out_sem,
    tile_sem,
    send_sem,
    recv_sem,
):
    chunks = kv_own.shape[0]
    o = lax.axis_index("outer")
    i = lax.axis_index("inner")
    core = lax.rem(i, 2)
    o_next, o_prev = lax.rem(o + 1, n_outer), lax.rem(o + n_outer - 1, n_outer)
    i_far, i_back = lax.rem(i + 2, n_inner), lax.rem(i + n_inner - 2, n_inner)
    to_next = (o_next, i)
    to_prev = (o_prev, i)
    to_far = (o_prev, i_far)
    to_back = (o_next, i_back)
    partner = (o, i + 1 - 2 * core)

    def remote(src, dst, kind, g, device):
        return pltpu.make_async_remote_copy(
            src_ref=src,
            dst_ref=dst,
            send_sem=send_sem.at[kind, g],
            recv_sem=recv_sem.at[kind, g],
            device_id=device,
            device_id_type=MESH,
        )

    def hop_group(g):
        return remote(kv_own.at[g], kv_grp.at[g], 0, g, to_next)

    def hop_far(g):
        return remote(kv_grp.at[g], kv_far.at[g], 1, g, to_far)

    def hop_near_own(g):
        return remote(kv_own.at[g], kv_near.at[g], 2, g, partner)

    def hop_near_far(g):
        return remote(kv_far.at[g], kv_near.at[g], 2, g, partner)

    def back_near(g):
        return remote(n_send.at[g], n_recv.at[g], 3, g, partner)

    def back_far(g):
        return remote(f_send.at[g], f_recv.at[g], 4, g, to_back)

    def back_sum(g):
        return remote(s_send.at[g], s_recv.at[g], 5, g, to_prev)

    def tile_copy(src, dst, kind, device):
        return pltpu.make_async_remote_copy(
            src_ref=tile.at[src],
            dst_ref=tile.at[dst],
            send_sem=tile_sem.at[0, kind],
            recv_sem=tile_sem.at[1, kind],
            device_id=device,
            device_id_type=MESH,
        )

    def load_kv(g):
        cols = pl.ds(g * HEAD_DIM, HEAD_DIM)
        return (
            pltpu.make_async_copy(k_hbm.at[:, cols], kv_own.at[g, 0], in_sem.at[0, g]),
            pltpu.make_async_copy(v_hbm.at[:, cols], kv_own.at[g, 1], in_sem.at[1, g]),
        )

    def load_q(g):
        cols = pl.ds(g * group * HEAD_DIM, group * HEAD_DIM)
        return (
            pltpu.make_async_copy(q_hbm.at[:, cols], q_v.at[g], in_sem.at[2, g]),
            pltpu.make_async_copy(do_hbm.at[:, cols], do_v.at[g], in_sem.at[3, g]),
        )

    def load_rows():
        return (
            pltpu.make_async_copy(lse_hbm, lse_v, in_sem.at[4, 0]),
            pltpu.make_async_copy(delta_hbm, delta_v, in_sem.at[4, 1]),
        )

    def store_q(g):
        cols = pl.ds(g * group * HEAD_DIM, group * HEAD_DIM)
        return pltpu.make_async_copy(gq_out.at[g], gq_hbm.at[:, cols], out_sem.at[0, g])

    def store_kv(g):
        cols = pl.ds(g * HEAD_DIM, HEAD_DIM)
        return (
            pltpu.make_async_copy(own32.at[g, 0], gk_hbm.at[:, cols], out_sem.at[1, g]),
            pltpu.make_async_copy(own32.at[g, 1], gv_hbm.at[:, cols], out_sem.at[2, g]),
        )

    for g in range(chunks):
        for copy in load_kv(g):
            copy.start()
    for copy in load_rows():
        copy.start()
    for g in range(chunks):
        for copy in load_q(g):
            copy.start()

    tile[0] = jnp.full(tile.shape[1:], piece_ref[0].astype(F32), F32)

    if COMM:
        barrier = pltpu.get_barrier_semaphore()
        for peer in (to_next, to_prev, to_far, to_back, partner):
            pl.semaphore_signal(barrier, inc=1, device_id=peer, device_id_type=MESH)
        pl.semaphore_wait(barrier, 5)
        tile_copy(0, 1, 0, to_next).start()

        @pl.when(core == 0)
        def _():
            tile_copy(0, 3, 2, partner).start()

    def send_own(g, carry):
        for copy in load_kv(g):
            copy.wait()
        if COMM:
            hop_group(g).start()

            @pl.when(core == 0)
            def _():
                hop_near_own(g).start()

        return carry

    lax.fori_loop(0, chunks, send_own, 0)
    for copy in load_rows():
        copy.wait()
    for g in range(chunks):
        lse_c[g] = lse_v[g * group : (g + 1) * group] * LOG2E
        delta_c[g] = delta_v[g * group : (g + 1) * group]

    def rows_of(ref, g, j, half):
        return ref[g, j : j + 1, half * HALF : (half + 1) * HALF]

    def head(ref, g, j, half):
        return ref[g, pl.ds(half * HALF, HALF), pl.ds(j * HEAD_DIM, HEAD_DIM)]

    def over_heads(parts):
        return jnp.concatenate(parts, axis=1)

    def own(g):
        keep = lax.broadcasted_iota(jnp.int32, (HALF, HALF), 0) <= lax.broadcasted_iota(
            jnp.int32, (HALF, HALF), 1
        )
        k0, k1 = kv_own[g, 0, :HALF], kv_own[g, 0, HALF:]
        v0, v1 = kv_own[g, 1, :HALF], kv_own[g, 1, HALF:]
        p_0, s_0, p_1, s_1 = [], [], [], []
        q_all, do_all = [], []
        for j in range(group):
            lse0 = rows_of(lse_c, g, j, 0)
            lse1 = rows_of(lse_c, g, j, 1)
            delta0 = rows_of(delta_c, g, j, 0)
            delta1 = rows_of(delta_c, g, j, 1)
            q0, q1 = head(q_v, g, j, 0), head(q_v, g, j, 1)
            do0, do1 = head(do_v, g, j, 0), head(do_v, g, j, 1)
            p00, s00 = quadrant(k0, v0, q0, do0, lse0, delta0, keep)
            p01, s01 = quadrant(k0, v0, q1, do1, lse1, delta1)
            p11, s11 = quadrant(k1, v1, q1, do1, lse1, delta1, keep)
            cols = pl.ds(j * HEAD_DIM, HEAD_DIM)
            gq_acc[g, :HALF, cols] = dot_nn(s00.T, k0)
            gq_acc[g, HALF:, cols] = dot_nn(
                jnp.concatenate([s01, s11], axis=0).T, kv_own[g, 0]
            )
            p_0 += [p00, p01]
            s_0 += [s00, s01]
            p_1.append(p11)
            s_1.append(s11)
            q_all += [q0, q1]
            do_all += [do0, do1]
        q_both = jnp.concatenate(q_all, axis=0)
        do_both = jnp.concatenate(do_all, axis=0)
        q_late = jnp.concatenate(q_all[1::2], axis=0)
        do_late = jnp.concatenate(do_all[1::2], axis=0)
        own32[g, 0, :HALF] = dot_nn(over_heads(s_0), q_both)
        own32[g, 0, HALF:] = dot_nn(over_heads(s_1), q_late)
        own32[g, 1, :HALF] = dot_nn(over_heads(p_0), do_both)
        own32[g, 1, HALF:] = dot_nn(over_heads(p_1), do_late)

    def other(g, kv_ref, which, out, as_type, last):
        early = flag[which] == 1
        k0, k1 = kv_ref[g, 0, :HALF], kv_ref[g, 0, HALF:]
        v0, v1 = kv_ref[g, 1, :HALF], kv_ref[g, 1, HALF:]
        kb, vb = jnp.where(early, k0, k1), jnp.where(early, v0, v1)
        p_a, s_a, p_b, s_b = [], [], [], []
        q_a, do_a, q_b, do_b = [], [], [], []
        for j in range(group):
            lse1 = rows_of(lse_c, g, j, 1)
            lseb = jnp.where(early, rows_of(lse_c, g, j, 0), lse1)
            delta1 = rows_of(delta_c, g, j, 1)
            deltab = jnp.where(early, rows_of(delta_c, g, j, 0), delta1)
            q1, do1 = head(q_v, g, j, 1), head(do_v, g, j, 1)
            qb = jnp.where(early, head(q_v, g, j, 0), q1)
            dob = jnp.where(early, head(do_v, g, j, 0), do1)
            pa, sa = quadrant(k0, v0, q1, do1, lse1, delta1)
            pb, sb = quadrant(kb, vb, qb, dob, lseb, deltab)
            gq_a, gq_b = dot_nn(sa.T, k0), dot_nn(sb.T, kb)
            cols = pl.ds(j * HEAD_DIM, HEAD_DIM)
            zero = jnp.zeros_like(gq_b)
            new0 = gq_acc[g, :HALF, cols] + jnp.where(early, gq_b, zero)
            new1 = gq_acc[g, HALF:, cols] + (gq_a + jnp.where(early, zero, gq_b))
            if last:
                gq_out[g, :HALF, cols] = (new0 * SCALE).astype(BF16)
                gq_out[g, HALF:, cols] = (new1 * SCALE).astype(BF16)
            else:
                gq_acc[g, :HALF, cols] = new0
                gq_acc[g, HALF:, cols] = new1
            p_a.append(pa)
            s_a.append(sa)
            p_b.append(pb)
            s_b.append(sb)
            q_a.append(q1)
            do_a.append(do1)
            q_b.append(qb)
            do_b.append(dob)
        for t, (xa, ya, xb, yb) in enumerate(((s_a, q_a, s_b, q_b), (p_a, do_a, p_b, do_b))):
            first = dot_nn(over_heads(xa), jnp.concatenate(ya, axis=0))
            second = dot_nn(over_heads(xb), jnp.concatenate(yb, axis=0))
            zero = jnp.zeros_like(second)
            out[g, t, :HALF] = (first + jnp.where(early, second, zero)).astype(as_type)
            out[g, t, HALF:] = jnp.where(early, zero, second).astype(as_type)

    def set_flag(which):
        mine = jnp.max(tile[0])
        flag[which] = (jnp.max(tile[which]) < mine).astype(jnp.int32)

    def step(t, carry):
        @pl.when(t < chunks)
        def _():
            g = t
            for copy in load_q(g):
                copy.wait()
            if COMPUTE:
                own(g)
            if COMM:
                hop_group(g).wait_recv()
                hop_far(g).start()

        if COMM:

            @pl.when(t == 0)
            def _():
                tile_copy(0, 1, 0, to_next).wait_recv()
                tile_copy(1, 2, 1, to_far).start()
                set_flag(1)

            @pl.when(t == 1)
            def _():
                tile_copy(1, 2, 1, to_far).wait_recv()

                @pl.when(core == 1)
                def _():
                    tile_copy(2, 3, 2, partner).start()

                set_flag(2)
                tile_copy(2, 3, 2, partner).wait_recv()
                set_flag(3)

        @pl.when((t >= 1) & (t < chunks + 1))
        def _():
            g = t - 1
            if COMM:
                hop_far(g).wait_recv()

                @pl.when(core == 1)
                def _():
                    hop_near_far(g).start()

                hop_near_own(g).wait_recv()
            if COMPUTE:
                other(g, kv_near, 3, n_send, BF16, False)
            if COMM:
                back_near(g).start()
            if COMPUTE:
                other(g, kv_far, 2, far32, F32, False)
                other(g, kv_grp, 1, grp32, F32, True)
            store_q(g).start()

        @pl.when((t >= 2) & (t < chunks + 2))
        def _():
            g = t - 2

            @pl.when(core == 0)
            def _():
                f_send[g] = far32[g].astype(BF16)

            @pl.when(core == 1)
            def _():
                if COMM:
                    back_near(g).wait_recv()
                f_send[g] = (far32[g] + n_recv[g].astype(F32)).astype(BF16)

            if COMM:
                back_far(g).start()

        @pl.when((t >= 3) & (t < chunks + 3))
        def _():
            g = t - 3
            if COMM:
                back_far(g).wait_recv()
            s_send[g] = (grp32[g] + f_recv[g].astype(F32)).astype(BF16)
            if COMM:
                back_sum(g).start()

        @pl.when((t >= 4) & (t < chunks + 4))
        def _():
            g = t - 4
            if COMM:
                back_sum(g).wait_recv()
            total = own32[g] + s_recv[g].astype(F32)

            @pl.when(core == 0)
            def _():
                if COMM:
                    back_near(g).wait_recv()
                both = total + n_recv[g].astype(F32)
                own32[g, 0] = both[0] * SCALE
                own32[g, 1] = both[1]

            @pl.when(core == 1)
            def _():
                own32[g, 0] = total[0] * SCALE
                own32[g, 1] = total[1]

            for copy in store_kv(g):
                copy.start()

        return carry

    lax.fori_loop(0, chunks + 4, step, 0)

    def drain(g, carry):
        store_q(g).wait()
        for copy in store_kv(g):
            copy.wait()
        if COMM:
            hop_group(g).wait_send()
            hop_far(g).wait_send()
            hop_near_own(g).wait_send()
            back_near(g).wait_send()
            back_far(g).wait_send()
            back_sum(g).wait_send()
        return carry

    lax.fori_loop(0, chunks, drain, 0)
    if COMM:
        tile_copy(0, 1, 0, to_next).wait_send()
        tile_copy(1, 2, 1, to_far).wait_send()
        tile_copy(0, 3, 2, partner).wait_send()


def on_device(n_outer, n_inner, queries, keys, values, grad_out, log_sum, row_delta, piece_index):
    rows = queries.shape[0]
    chunks = keys.shape[1] // HEAD_DIM
    group = queries.shape[1] // keys.shape[1]
    wide = (chunks, rows, group * HEAD_DIM)
    pair = (chunks, 2, rows, HEAD_DIM)
    hbm = pl.BlockSpec(memory_space=pl.ANY)
    vmem = pltpu.VMEM
    return pl.pallas_call(
        functools.partial(kernel, group, n_outer, n_inner),
        out_shape=(
            jax.ShapeDtypeStruct(queries.shape, BF16),
            jax.ShapeDtypeStruct(keys.shape, F32),
            jax.ShapeDtypeStruct(values.shape, F32),
        ),
        in_specs=[hbm] * 6 + [pl.BlockSpec(memory_space=pltpu.SMEM)],
        out_specs=(hbm, hbm, hbm),
        scratch_shapes=[
            vmem(wide, BF16),
            vmem(wide, BF16),
            vmem(log_sum.shape, F32),
            vmem(row_delta.shape, F32),
            vmem((chunks, group, rows), F32),
            vmem((chunks, group, rows), F32),
            vmem(pair, BF16),
            vmem(pair, BF16),
            vmem(pair, BF16),
            vmem(pair, BF16),
            vmem(wide, F32),
            vmem(wide, BF16),
            vmem(pair, F32),
            vmem(pair, F32),
            vmem(pair, F32),
            vmem(pair, BF16),
            vmem(pair, BF16),
            vmem(pair, BF16),
            vmem(pair, BF16),
            vmem(pair, BF16),
            vmem(pair, BF16),
            vmem((4, 8, 128), F32),
            pltpu.SMEM((4,), jnp.int32),
            pltpu.SemaphoreType.DMA((5, chunks)),
            pltpu.SemaphoreType.DMA((3, chunks)),
            pltpu.SemaphoreType.DMA((2, 3)),
            pltpu.SemaphoreType.DMA((6, chunks)),
            pltpu.SemaphoreType.DMA((6, chunks)),
        ],
        compiler_params=pltpu.CompilerParams(
            collective_id=0 if COMM else None, has_side_effects=True, vmem_limit_bytes=48 * 1024 * 1024
        ),
        cost_estimate=pl.CostEstimate(
            flops=6_000_000_000, bytes_accessed=10_000_000, transcendentals=5_000_000
        ),
    )(queries, keys, values, grad_out, log_sum, row_delta, piece_index)


def solution(mesh):
    in_specs = (
        P(("outer", "inner"), None),
        P(("outer", "inner"), None),
        P(("outer", "inner"), None),
        P(("outer", "inner"), None),
        P(None, ("outer", "inner")),
        P(None, ("outer", "inner")),
        P(("outer", "inner")),
    )
    out_specs = (
        P(("outer", "inner"), None),
        P(("outer", "inner"), None),
        P(("outer", "inner"), None),
    )
    body = functools.partial(on_device, mesh.shape["outer"], mesh.shape["inner"])
    return jax.shard_map(
        body, mesh=mesh, in_specs=in_specs, out_specs=out_specs, check_vma=False
    )
```

```python
import functools
import math

import jax
import jax.numpy as jnp
from jax import lax
from jax.experimental import pallas as pl
from jax.experimental.pallas import tpu as pltpu
from jax.sharding import PartitionSpec as P

HEAD_DIM = 128
HALF = 128
MESH = pl.DeviceIdType.MESH
SCALE = 1.0 / math.sqrt(HEAD_DIM)
LOG2E = math.log2(math.e)
COMM = True
LEAD = 4
COMPUTE = True

BF16 = jnp.bfloat16
F32 = jnp.float32


def dot_nt(a, b):
    return lax.dot_general(a, b, (((1,), (1,)), ((), ())), preferred_element_type=F32)


def dot_nn(a, b):
    return lax.dot_general(a, b, (((1,), (0,)), ((), ())), preferred_element_type=F32)


def quadrant(k, v, q, do, lse2, delta, keep=None):
    p = jnp.exp2(dot_nt(k, q) * (SCALE * LOG2E) - lse2)
    if keep is not None:
        p = jnp.where(keep, p, 0.0)
    ds = p * (dot_nt(v, do) - delta)
    return p.astype(BF16), ds.astype(BF16)


def kernel(
    group,
    n_outer,
    n_inner,
    q_hbm,
    k_hbm,
    v_hbm,
    do_hbm,
    lse_hbm,
    delta_hbm,
    piece_ref,
    gq_hbm,
    gk_hbm,
    gv_hbm,
    k_v,
    v_v,
    q_v,
    do_v,
    lse_v,
    delta_v,
    lse_c,
    delta_c,
    kv_own,
    kv_hop,
    kv_far,
    kv_near,
    gq_own,
    gq_acc,
    gq_out,
    own32,
    n_send,
    n_recv,
    f_send,
    f_recv,
    g_send,
    g_recv,
    s_send,
    s_recv,
    tile,
    flag,
    in_sem,
    out_sem,
    tile_sem,
    send_sem,
    recv_sem,
):
    chunks = kv_own.shape[0]
    o = lax.axis_index("outer")
    i = lax.axis_index("inner")
    core = lax.rem(i, 2)
    odd = lax.rem(o, 2)
    o_pair = o + 1 - 2 * odd
    i_far, i_back = lax.rem(i + 2, n_inner), lax.rem(i + n_inner - 2, n_inner)
    to_pair = (o_pair, i)
    to_far = (o_pair, i_far)
    to_back = (o_pair, i_back)
    to_up = (lax.rem(o + 2, n_outer), i)
    to_down = (lax.rem(o + n_outer - 2, n_outer), i)
    partner = (o, i + 1 - 2 * core)
    kv_grp = kv_hop.at[0]

    def remote(src, dst, kind, g, device):
        return pltpu.make_async_remote_copy(
            src_ref=src,
            dst_ref=dst,
            send_sem=send_sem.at[kind, g],
            recv_sem=recv_sem.at[kind, g],
            device_id=device,
            device_id_type=MESH,
        )

    def hop_pair(g):
        return remote(kv_own.at[g], kv_hop.at[odd, g], 0, g, to_pair)

    def hop_far(g):
        return remote(kv_hop.at[1 - odd, g], kv_far.at[g], 1, g, to_far)

    def hop_up(g):
        return remote(kv_hop.at[1, g], kv_hop.at[0, g], 6, g, to_up)

    def hop_near_own(g):
        return remote(kv_own.at[g], kv_near.at[g], 2, g, partner)

    def hop_near_far(g):
        return remote(kv_far.at[g], kv_near.at[g], 2, g, partner)

    def back_near(g):
        return remote(n_send.at[g], n_recv.at[g], 3, g, partner)

    def back_far(g):
        return remote(f_send.at[g], f_recv.at[g], 4, g, to_back)

    def back_sum(g):
        return remote(s_send.at[g], s_recv.at[g], 5, g, to_pair)

    def back_down(g):
        return remote(g_send.at[g], g_recv.at[g], 7, g, to_down)

    def tile_copy(src, dst, kind, device):
        return pltpu.make_async_remote_copy(
            src_ref=tile.at[src],
            dst_ref=tile.at[dst],
            send_sem=tile_sem.at[0, kind],
            recv_sem=tile_sem.at[1, kind],
            device_id=device,
            device_id_type=MESH,
        )

    def tile_pair():
        return tile_copy(0, 1 + 3 * odd, 0, to_pair)

    def tile_far():
        return tile_copy(4 - 3 * odd, 2, 1, to_far)

    def tile_near():
        return tile_copy(2 * core, 3, 2, partner)

    def tile_up():
        return tile_copy(4, 1, 3, to_up)

    def load_kv():
        return (
            pltpu.make_async_copy(k_hbm, k_v, in_sem.at[0, 0]),
            pltpu.make_async_copy(v_hbm, v_v, in_sem.at[1, 0]),
        )

    def load_q(g):
        cols = pl.ds(g * group * HEAD_DIM, group * HEAD_DIM)
        return (
            pltpu.make_async_copy(q_hbm.at[:, cols], q_v.at[g], in_sem.at[2, g]),
            pltpu.make_async_copy(do_hbm.at[:, cols], do_v.at[g], in_sem.at[3, g]),
        )

    def load_rows():
        return (
            pltpu.make_async_copy(lse_hbm, lse_v, in_sem.at[4, 0]),
            pltpu.make_async_copy(delta_hbm, delta_v, in_sem.at[4, 1]),
        )

    def store_q(g):
        cols = pl.ds(g * group * HEAD_DIM, group * HEAD_DIM)
        return pltpu.make_async_copy(gq_out.at[g], gq_hbm.at[:, cols], out_sem.at[0, g])

    def store_kv(g):
        cols = pl.ds(g * HEAD_DIM, HEAD_DIM)
        return (
            pltpu.make_async_copy(own32.at[g, 0], gk_hbm.at[:, cols], out_sem.at[1, g]),
            pltpu.make_async_copy(own32.at[g, 1], gv_hbm.at[:, cols], out_sem.at[2, g]),
        )

    for copy in load_kv():
        copy.start()
    for copy in load_rows():
        copy.start()
    for g in range(chunks):
        for copy in load_q(g):
            copy.start()

    tile[0] = jnp.full(tile.shape[1:], piece_ref[0].astype(F32), F32)

    if COMM:
        barrier = pltpu.get_barrier_semaphore()
        for peer in (to_pair, to_far, to_back, partner):
            pl.semaphore_signal(barrier, inc=1, device_id=peer, device_id_type=MESH)

        @pl.when(odd == 0)
        def _():
            for peer in (to_up, to_down):
                pl.semaphore_signal(barrier, inc=1, device_id=peer, device_id_type=MESH)
            pl.semaphore_wait(barrier, 6)

        @pl.when(odd == 1)
        def _():
            pl.semaphore_wait(barrier, 4)

        tile_pair().start()

        @pl.when(core == 0)
        def _():
            tile_near().start()

    def send_own(g, carry):
        if COMM:
            hop_pair(g).start()

            @pl.when(core == 0)
            def _():
                hop_near_own(g).start()

        return carry

    for copy in load_kv():
        copy.wait()
    for g in range(chunks):
        kv_own[g, 0] = k_v[:, g * HEAD_DIM : (g + 1) * HEAD_DIM]
        kv_own[g, 1] = v_v[:, g * HEAD_DIM : (g + 1) * HEAD_DIM]
    lax.fori_loop(0, LEAD, send_own, 0)
    for copy in load_rows() + load_q(0):
        copy.wait()
    for g in range(chunks):
        lse_c[g] = lse_v[g * group : (g + 1) * group] * LOG2E
        delta_c[g] = delta_v[g * group : (g + 1) * group]

    def rows_of(ref, g, j, half):
        return ref[g, j : j + 1, half * HALF : (half + 1) * HALF]

    def head(ref, g, j, half):
        return ref[g, pl.ds(half * HALF, HALF), pl.ds(j * HEAD_DIM, HEAD_DIM)]

    def over_heads(parts):
        return jnp.concatenate(parts, axis=1)

    def own(g):
        keep = lax.broadcasted_iota(jnp.int32, (HALF, HALF), 0) <= lax.broadcasted_iota(
            jnp.int32, (HALF, HALF), 1
        )
        k0, k1 = kv_own[g, 0, :HALF], kv_own[g, 0, HALF:]
        v0, v1 = kv_own[g, 1, :HALF], kv_own[g, 1, HALF:]
        p_0, s_0, p_1, s_1 = [], [], [], []
        q_all, do_all = [], []
        for j in range(group):
            lse0 = rows_of(lse_c, g, j, 0)
            lse1 = rows_of(lse_c, g, j, 1)
            delta0 = rows_of(delta_c, g, j, 0)
            delta1 = rows_of(delta_c, g, j, 1)
            q0, q1 = head(q_v, g, j, 0), head(q_v, g, j, 1)
            do0, do1 = head(do_v, g, j, 0), head(do_v, g, j, 1)
            p00, s00 = quadrant(k0, v0, q0, do0, lse0, delta0, keep)
            p01, s01 = quadrant(k0, v0, q1, do1, lse1, delta1)
            p11, s11 = quadrant(k1, v1, q1, do1, lse1, delta1, keep)
            p_0 += [p00, p01]
            s_0 += [s00, s01]
            p_1.append(p11)
            s_1.append(s11)
            q_all += [q0, q1]
            do_all += [do0, do1]
        early = dot_nn(over_heads(s_0[0::2]).T, k0)
        late = dot_nn(
            jnp.concatenate([over_heads(s_0[1::2]).T, over_heads(s_1).T], axis=1), kv_own[g, 0]
        )
        for j in range(group):
            cols = pl.ds(j * HEAD_DIM, HEAD_DIM)
            gq_own[g, :HALF, cols] = early[j * HALF : (j + 1) * HALF]
            gq_own[g, HALF:, cols] = late[j * HALF : (j + 1) * HALF]
        q_both = jnp.concatenate(q_all, axis=0)
        do_both = jnp.concatenate(do_all, axis=0)
        q_late = jnp.concatenate(q_all[1::2], axis=0)
        do_late = jnp.concatenate(do_all[1::2], axis=0)
        own32[g, 0, :HALF] = dot_nn(over_heads(s_0), q_both)
        own32[g, 0, HALF:] = dot_nn(over_heads(s_1), q_late)
        own32[g, 1, :HALF] = dot_nn(over_heads(p_0), do_both)
        own32[g, 1, HALF:] = dot_nn(over_heads(p_1), do_late)

    def other(g, kv_ref, which, out, first):
        early = flag[which] == 1
        k0, k1 = kv_ref[g, 0, :HALF], kv_ref[g, 0, HALF:]
        v0, v1 = kv_ref[g, 1, :HALF], kv_ref[g, 1, HALF:]
        kb, vb = jnp.where(early, k0, k1), jnp.where(early, v0, v1)
        p_a, s_a, p_b, s_b = [], [], [], []
        q_a, do_a, q_b, do_b = [], [], [], []
        for j in range(group):
            lse1 = rows_of(lse_c, g, j, 1)
            lseb = jnp.where(early, rows_of(lse_c, g, j, 0), lse1)
            delta1 = rows_of(delta_c, g, j, 1)
            deltab = jnp.where(early, rows_of(delta_c, g, j, 0), delta1)
            q1, do1 = head(q_v, g, j, 1), head(do_v, g, j, 1)
            qb = jnp.where(early, head(q_v, g, j, 0), q1)
            dob = jnp.where(early, head(do_v, g, j, 0), do1)
            pa, sa = quadrant(k0, v0, q1, do1, lse1, delta1)
            pb, sb = quadrant(kb, vb, qb, dob, lseb, deltab)
            p_a.append(pa)
            s_a.append(sa)
            p_b.append(pb)
            s_b.append(sb)
            q_a.append(q1)
            do_a.append(do1)
            q_b.append(qb)
            do_b.append(dob)
        blank = jnp.zeros_like(k0)
        weights = jnp.concatenate(
            [jnp.concatenate([k0, blank], axis=1), jnp.concatenate([blank, kb], axis=1)], axis=0
        )
        both = dot_nn(jnp.concatenate([over_heads(s_a).T, over_heads(s_b).T], axis=1), weights)
        for j in range(group):
            cols = pl.ds(j * HEAD_DIM, HEAD_DIM)
            gq_a = both[j * HALF : (j + 1) * HALF, :HEAD_DIM]
            gq_b = both[j * HALF : (j + 1) * HALF, HEAD_DIM:]
            zero = jnp.zeros_like(gq_b)
            add0 = jnp.where(early, gq_b, zero)
            add1 = gq_a + jnp.where(early, zero, gq_b)
            if first:
                gq_acc[g, :HALF, cols] = add0
                gq_acc[g, HALF:, cols] = add1
            else:
                gq_acc[g, :HALF, cols] += add0
                gq_acc[g, HALF:, cols] += add1
        for t, (xa, ya, xb, yb) in enumerate(((s_a, q_a, s_b, q_b), (p_a, do_a, p_b, do_b))):
            one = dot_nn(over_heads(xa), jnp.concatenate(ya, axis=0))
            second = dot_nn(over_heads(xb), jnp.concatenate(yb, axis=0))
            zero = jnp.zeros_like(second)
            out[g, t, :HALF] = (one + jnp.where(early, second, zero)).astype(BF16)
            out[g, t, HALF:] = jnp.where(early, zero, second).astype(BF16)

    def set_flag(which):
        mine = jnp.max(tile[0])
        flag[which] = (jnp.max(tile[which]) < mine).astype(jnp.int32)

    if COMPUTE:
        own(0)
    for g in range(1, chunks):
        for copy in load_q(g):
            copy.wait()

    def step(t, carry):
        @pl.when(t < chunks)
        def _():
            g = t
            if COMM:
                hop_pair(g).wait_recv()
                hop_far(g).start()

            @pl.when(g + LEAD < chunks)
            def _():
                send_own(g + LEAD, 0)

            if COMM:

                @pl.when(odd == 0)
                def _():
                    hop_up(g).start()

        if COMM:

            @pl.when(t == 0)
            def _():
                tile_pair().wait_recv()
                tile_far().start()

                @pl.when(odd == 0)
                def _():
                    tile_up().start()

            @pl.when(t == 1)
            def _():
                tile_far().wait_recv()

                @pl.when(core == 1)
                def _():
                    tile_near().start()

        @pl.when((t >= 2) & (t < chunks + 2))
        def _():
            g = t - 2
            if COMM:
                hop_far(g).wait_recv()

                @pl.when(core == 1)
                def _():
                    hop_near_far(g).start()

        if COMM:

            @pl.when(t == 3)
            def _():
                @pl.when(odd == 0)
                def _():
                    tile_up().wait_recv()

                tile_near().wait_recv()
                for which in (1, 2, 3):
                    set_flag(which)

        @pl.when((t >= 3) & (t < chunks + 3))
        def _():
            g = t - 3
            if COMM:
                hop_near_own(g).wait_recv()
            if COMPUTE:
                other(g, kv_near, 3, n_send, True)
            if COMM:
                back_near(g).start()
            if COMPUTE:
                other(g, kv_far, 2, f_send, False)
            if COMM:

                @pl.when(core == 0)
                def _():
                    back_far(g).start()

                @pl.when(odd == 0)
                def _():
                    hop_up(g).wait_recv()

            if COMPUTE:
                other(g, kv_grp, 1, g_send, False)
            if COMM:

                @pl.when(odd == 0)
                def _():
                    back_down(g).start()

        if COMM:

            @pl.when((t >= 4) & (t < chunks + 4) & (core == 1))
            def _():
                g = t - 4
                back_near(g).wait_recv()
                f_send[g] = (f_send[g].astype(F32) + n_recv[g].astype(F32)).astype(BF16)
                back_far(g).start()

        if COMPUTE:
            @pl.when(t < 3)
            def _():
                own(t + 1)

            @pl.when((t >= chunks + 3) & (t < 2 * chunks - 1))
            def _():
                own(t + 1 - chunks)

        if COMM:

            @pl.when((t >= 6) & (t < chunks + 6))
            def _():
                g = t - 6
                back_far(g).wait_recv()

                @pl.when(odd == 0)
                def _():
                    back_down(g).wait_recv()
                    s_send[g] = (f_recv[g].astype(F32) + g_recv[g].astype(F32)).astype(BF16)

                @pl.when(odd == 1)
                def _():
                    s_send[g] = (f_recv[g].astype(F32) + g_send[g].astype(F32)).astype(BF16)

                back_sum(g).start()

        @pl.when(t >= 8)
        def _():
            g = t - 8
            gq_out[g] = ((gq_own[g] + gq_acc[g]) * SCALE).astype(BF16)
            store_q(g).start()
            if COMM:
                back_sum(g).wait_recv()
            total = own32[g] + s_recv[g].astype(F32)

            @pl.when(core == 0)
            def _():
                if COMM:
                    back_near(g).wait_recv()
                both = total + n_recv[g].astype(F32)
                own32[g, 0] = both[0] * SCALE
                own32[g, 1] = both[1]

            @pl.when(core == 1)
            def _():
                own32[g, 0] = total[0] * SCALE
                own32[g, 1] = total[1]

            for copy in store_kv(g):
                copy.start()

        return carry

    lax.fori_loop(0, chunks + 8, step, 0)

    def drain(g, carry):
        store_q(g).wait()
        for copy in store_kv(g):
            copy.wait()
        if COMM:
            hop_pair(g).wait_send()
            hop_far(g).wait_send()
            hop_near_own(g).wait_send()
            back_near(g).wait_send()
            back_far(g).wait_send()
            back_sum(g).wait_send()

            @pl.when(odd == 0)
            def _():
                hop_up(g).wait_send()
                back_down(g).wait_send()

        return carry

    lax.fori_loop(0, chunks, drain, 0)
    if COMM:
        tile_pair().wait_send()
        tile_far().wait_send()
        tile_near().wait_send()

        @pl.when(odd == 0)
        def _():
            tile_up().wait_send()


def on_device(n_outer, n_inner, queries, keys, values, grad_out, log_sum, row_delta, piece_index):
    rows = queries.shape[0]
    chunks = keys.shape[1] // HEAD_DIM
    group = queries.shape[1] // keys.shape[1]
    wide = (chunks, rows, group * HEAD_DIM)
    pair = (chunks, 2, rows, HEAD_DIM)
    hbm = pl.BlockSpec(memory_space=pltpu.HBM)
    vmem = pltpu.VMEM
    return pl.pallas_call(
        functools.partial(kernel, group, n_outer, n_inner),
        out_shape=(
            jax.ShapeDtypeStruct(queries.shape, BF16),
            jax.ShapeDtypeStruct(keys.shape, F32),
            jax.ShapeDtypeStruct(values.shape, F32),
        ),
        in_specs=[hbm] * 6 + [pl.BlockSpec(memory_space=pltpu.SMEM)],
        out_specs=(hbm, hbm, hbm),
        scratch_shapes=[
            vmem(keys.shape, BF16),
            vmem(values.shape, BF16),
            vmem(wide, BF16),
            vmem(wide, BF16),
            vmem(log_sum.shape, F32),
            vmem(row_delta.shape, F32),
            vmem((chunks, group, rows), F32),
            vmem((chunks, group, rows), F32),
            vmem(pair, BF16),
            vmem((2,) + pair, BF16),
            vmem(pair, BF16),
            vmem(pair, BF16),
            vmem(wide, F32),
            vmem(wide, F32),
            vmem(wide, BF16),
            vmem(pair, F32),
            vmem(pair, BF16),
            vmem(pair, BF16),
            vmem(pair, BF16),
            vmem(pair, BF16),
            vmem(pair, BF16),
            vmem(pair, BF16),
            vmem(pair, BF16),
            vmem(pair, BF16),
            vmem((5, 8, 128), F32),
            pltpu.SMEM((4,), jnp.int32),
            pltpu.SemaphoreType.DMA((5, chunks)),
            pltpu.SemaphoreType.DMA((3, chunks)),
            pltpu.SemaphoreType.DMA((2, 4)),
            pltpu.SemaphoreType.DMA((8, chunks)),
            pltpu.SemaphoreType.DMA((8, chunks)),
        ],
        compiler_params=pltpu.CompilerParams(
            collective_id=0 if COMM else None, has_side_effects=True, vmem_limit_bytes=56 * 1024 * 1024
        ),
        cost_estimate=pl.CostEstimate(
            flops=6_000_000_000, bytes_accessed=10_000_000, transcendentals=5_000_000
        ),
    )(queries, keys, values, grad_out, log_sum, row_delta, piece_index)


def solution(mesh):
    in_specs = (
        P(("outer", "inner"), None),
        P(("outer", "inner"), None),
        P(("outer", "inner"), None),
        P(("outer", "inner"), None),
        P(None, ("outer", "inner")),
        P(None, ("outer", "inner")),
        P(("outer", "inner")),
    )
    out_specs = (
        P(("outer", "inner"), None),
        P(("outer", "inner"), None),
        P(("outer", "inner"), None),
    )
    body = functools.partial(on_device, mesh.shape["outer"], mesh.shape["inner"])
    return jax.shard_map(
        body, mesh=mesh, in_specs=in_specs, out_specs=out_specs, check_vma=False
    )
```

```python
import functools
import math

import jax
import jax.numpy as jnp
from jax import lax
from jax.experimental import pallas as pl
from jax.experimental.pallas import tpu as pltpu
from jax.sharding import PartitionSpec as P

HEAD_DIM = 128
HALF = 128
MESH = pl.DeviceIdType.MESH
SCALE = 1.0 / math.sqrt(HEAD_DIM)
LOG2E = math.log2(math.e)
COMM = True
LEAD = 4
COMPUTE = True

BF16 = jnp.bfloat16
F32 = jnp.float32


def dot_nt(a, b):
    return lax.dot_general(a, b, (((1,), (1,)), ((), ())), preferred_element_type=F32)


def dot_nn(a, b):
    return lax.dot_general(a, b, (((1,), (0,)), ((), ())), preferred_element_type=F32)


def quadrant(k, v, q, do, lse2, delta, keep=None):
    p = jnp.exp2(dot_nt(k, q) * (SCALE * LOG2E) - lse2)
    if keep is not None:
        p = jnp.where(keep, p, 0.0)
    ds = p * (dot_nt(v, do) - delta)
    return p.astype(BF16), ds.astype(BF16)


def kernel(
    group,
    n_outer,
    n_inner,
    q_hbm,
    k_hbm,
    v_hbm,
    do_hbm,
    lse_hbm,
    delta_hbm,
    piece_ref,
    gq_hbm,
    gk_hbm,
    gv_hbm,
    k_v,
    v_v,
    q_v,
    do_v,
    lse_v,
    delta_v,
    lse_c,
    delta_c,
    kv_own,
    kv_hop,
    kv_far,
    kv_near,
    gq_own,
    gq_acc,
    gq_out,
    own32,
    n_send,
    n_recv,
    f_send,
    f_recv,
    g_send,
    g_recv,
    s_send,
    s_recv,
    tile,
    flag,
    in_sem,
    out_sem,
    tile_sem,
    send_sem,
    recv_sem,
):
    chunks = kv_own.shape[0]
    o = lax.axis_index("outer")
    i = lax.axis_index("inner")
    core = lax.rem(i, 2)
    odd = lax.rem(o, 2)
    o_pair = o + 1 - 2 * odd
    i_far, i_back = lax.rem(i + 2, n_inner), lax.rem(i + n_inner - 2, n_inner)
    to_pair = (o_pair, i)
    to_far = (o_pair, i_far)
    to_back = (o_pair, i_back)
    to_up = (lax.rem(o + 2, n_outer), i)
    to_down = (lax.rem(o + n_outer - 2, n_outer), i)
    partner = (o, i + 1 - 2 * core)
    kv_grp = kv_hop.at[0]

    def remote(src, dst, kind, g, device):
        return pltpu.make_async_remote_copy(
            src_ref=src,
            dst_ref=dst,
            send_sem=send_sem.at[kind, g],
            recv_sem=recv_sem.at[kind, g],
            device_id=device,
            device_id_type=MESH,
        )

    def hop_pair(g, x):
        return remote(kv_own.at[g, x], kv_hop.at[odd, g, x], 8 * x, g, to_pair)

    def hop_far(g, x):
        return remote(kv_hop.at[1 - odd, g, x], kv_far.at[g, x], 1 + 8 * x, g, to_far)

    def hop_up(g):
        return remote(kv_hop.at[1, g], kv_hop.at[0, g], 6, g, to_up)

    def hop_near_own(g):
        return remote(kv_own.at[g], kv_near.at[g], 2, g, partner)

    def hop_near_far(g):
        return remote(kv_far.at[g], kv_near.at[g], 2, g, partner)

    def back_near(g):
        return remote(n_send.at[g], n_recv.at[g], 3, g, partner)

    def back_far(g):
        return remote(f_send.at[g], f_recv.at[g], 4, g, to_back)

    def back_sum(g):
        return remote(s_send.at[g], s_recv.at[g], 5, g, to_pair)

    def back_down(g):
        return remote(g_send.at[g], g_recv.at[g], 7, g, to_down)

    def tile_copy(src, dst, kind, device):
        return pltpu.make_async_remote_copy(
            src_ref=tile.at[src],
            dst_ref=tile.at[dst],
            send_sem=tile_sem.at[0, kind],
            recv_sem=tile_sem.at[1, kind],
            device_id=device,
            device_id_type=MESH,
        )

    def tile_pair():
        return tile_copy(0, 1 + 3 * odd, 0, to_pair)

    def tile_far():
        return tile_copy(4 - 3 * odd, 2, 1, to_far)

    def tile_near():
        return tile_copy(2 * core, 3, 2, partner)

    def tile_up():
        return tile_copy(4, 1, 3, to_up)

    def load_kv():
        return (
            pltpu.make_async_copy(k_hbm, k_v, in_sem.at[0, 0]),
            pltpu.make_async_copy(v_hbm, v_v, in_sem.at[1, 0]),
        )

    def load_q(g):
        cols = pl.ds(g * group * HEAD_DIM, group * HEAD_DIM)
        return (
            pltpu.make_async_copy(q_hbm.at[:, cols], q_v.at[g], in_sem.at[2, g]),
            pltpu.make_async_copy(do_hbm.at[:, cols], do_v.at[g], in_sem.at[3, g]),
        )

    def load_rows():
        return (
            pltpu.make_async_copy(lse_hbm, lse_v, in_sem.at[4, 0]),
            pltpu.make_async_copy(delta_hbm, delta_v, in_sem.at[4, 1]),
        )

    def store_q(g):
        cols = pl.ds(g * group * HEAD_DIM, group * HEAD_DIM)
        return pltpu.make_async_copy(gq_out.at[g], gq_hbm.at[:, cols], out_sem.at[0, g])

    def store_kv(g):
        cols = pl.ds(g * HEAD_DIM, HEAD_DIM)
        return (
            pltpu.make_async_copy(own32.at[g, 0], gk_hbm.at[:, cols], out_sem.at[1, g]),
            pltpu.make_async_copy(own32.at[g, 1], gv_hbm.at[:, cols], out_sem.at[2, g]),
        )

    for copy in load_kv():
        copy.start()
    for copy in load_rows():
        copy.start()
    for g in range(chunks):
        for copy in load_q(g):
            copy.start()

    tile[0] = jnp.full(tile.shape[1:], piece_ref[0].astype(F32), F32)

    if COMM:
        barrier = pltpu.get_barrier_semaphore()
        for peer in (to_pair, to_far, to_back, partner):
            pl.semaphore_signal(barrier, inc=1, device_id=peer, device_id_type=MESH)

        @pl.when(odd == 0)
        def _():
            for peer in (to_up, to_down):
                pl.semaphore_signal(barrier, inc=1, device_id=peer, device_id_type=MESH)
            pl.semaphore_wait(barrier, 6)

        @pl.when(odd == 1)
        def _():
            pl.semaphore_wait(barrier, 4)

        tile_pair().start()

        @pl.when(core == 0)
        def _():
            tile_near().start()

    def send_own(g, carry):
        if COMM:
            for x in range(2):
                hop_pair(g, x).start()

            @pl.when(core == 0)
            def _():
                hop_near_own(g).start()

        return carry

    for copy in load_kv():
        copy.wait()
    for g in range(chunks):
        kv_own[g, 0] = k_v[:, g * HEAD_DIM : (g + 1) * HEAD_DIM]
        kv_own[g, 1] = v_v[:, g * HEAD_DIM : (g + 1) * HEAD_DIM]
    lax.fori_loop(0, LEAD, send_own, 0)
    for copy in load_rows() + load_q(0):
        copy.wait()
    for g in range(chunks):
        lse_c[g] = lse_v[g * group : (g + 1) * group] * LOG2E
        delta_c[g] = delta_v[g * group : (g + 1) * group]

    def rows_of(ref, g, j, half):
        return ref[g, j : j + 1, half * HALF : (half + 1) * HALF]

    def head(ref, g, j, half):
        return ref[g, pl.ds(half * HALF, HALF), pl.ds(j * HEAD_DIM, HEAD_DIM)]

    def over_heads(parts):
        return jnp.concatenate(parts, axis=1)

    def own(g):
        keep = lax.broadcasted_iota(jnp.int32, (HALF, HALF), 0) <= lax.broadcasted_iota(
            jnp.int32, (HALF, HALF), 1
        )
        k0, k1 = kv_own[g, 0, :HALF], kv_own[g, 0, HALF:]
        v0, v1 = kv_own[g, 1, :HALF], kv_own[g, 1, HALF:]
        p_0, s_0, p_1, s_1 = [], [], [], []
        q_all, do_all = [], []
        for j in range(group):
            lse0 = rows_of(lse_c, g, j, 0)
            lse1 = rows_of(lse_c, g, j, 1)
            delta0 = rows_of(delta_c, g, j, 0)
            delta1 = rows_of(delta_c, g, j, 1)
            q0, q1 = head(q_v, g, j, 0), head(q_v, g, j, 1)
            do0, do1 = head(do_v, g, j, 0), head(do_v, g, j, 1)
            p00, s00 = quadrant(k0, v0, q0, do0, lse0, delta0, keep)
            p01, s01 = quadrant(k0, v0, q1, do1, lse1, delta1)
            p11, s11 = quadrant(k1, v1, q1, do1, lse1, delta1, keep)
            p_0 += [p00, p01]
            s_0 += [s00, s01]
            p_1.append(p11)
            s_1.append(s11)
            q_all += [q0, q1]
            do_all += [do0, do1]
        early = dot_nn(over_heads(s_0[0::2]).T, k0)
        late = dot_nn(
            jnp.concatenate([over_heads(s_0[1::2]).T, over_heads(s_1).T], axis=1), kv_own[g, 0]
        )
        for j in range(group):
            cols = pl.ds(j * HEAD_DIM, HEAD_DIM)
            gq_own[g, :HALF, cols] = early[j * HALF : (j + 1) * HALF]
            gq_own[g, HALF:, cols] = late[j * HALF : (j + 1) * HALF]
        q_both = jnp.concatenate(q_all, axis=0)
        do_both = jnp.concatenate(do_all, axis=0)
        q_late = jnp.concatenate(q_all[1::2], axis=0)
        do_late = jnp.concatenate(do_all[1::2], axis=0)
        own32[g, 0, :HALF] = dot_nn(over_heads(s_0), q_both)
        own32[g, 0, HALF:] = dot_nn(over_heads(s_1), q_late)
        own32[g, 1, :HALF] = dot_nn(over_heads(p_0), do_both)
        own32[g, 1, HALF:] = dot_nn(over_heads(p_1), do_late)

    def other(g, kv_ref, which, out, first):
        early = flag[which] == 1
        k0, k1 = kv_ref[g, 0, :HALF], kv_ref[g, 0, HALF:]
        v0, v1 = kv_ref[g, 1, :HALF], kv_ref[g, 1, HALF:]
        kb, vb = jnp.where(early, k0, k1), jnp.where(early, v0, v1)
        p_a, s_a, p_b, s_b = [], [], [], []
        q_a, do_a, q_b, do_b = [], [], [], []
        for j in range(group):
            lse1 = rows_of(lse_c, g, j, 1)
            lseb = jnp.where(early, rows_of(lse_c, g, j, 0), lse1)
            delta1 = rows_of(delta_c, g, j, 1)
            deltab = jnp.where(early, rows_of(delta_c, g, j, 0), delta1)
            q1, do1 = head(q_v, g, j, 1), head(do_v, g, j, 1)
            qb = jnp.where(early, head(q_v, g, j, 0), q1)
            dob = jnp.where(early, head(do_v, g, j, 0), do1)
            pa, sa = quadrant(k0, v0, q1, do1, lse1, delta1)
            pb, sb = quadrant(kb, vb, qb, dob, lseb, deltab)
            p_a.append(pa)
            s_a.append(sa)
            p_b.append(pb)
            s_b.append(sb)
            q_a.append(q1)
            do_a.append(do1)
            q_b.append(qb)
            do_b.append(dob)
        blank = jnp.zeros_like(k0)
        weights = jnp.concatenate(
            [jnp.concatenate([k0, blank], axis=1), jnp.concatenate([blank, kb], axis=1)], axis=0
        )
        both = dot_nn(jnp.concatenate([over_heads(s_a).T, over_heads(s_b).T], axis=1), weights)
        for j in range(group):
            cols = pl.ds(j * HEAD_DIM, HEAD_DIM)
            gq_a = both[j * HALF : (j + 1) * HALF, :HEAD_DIM]
            gq_b = both[j * HALF : (j + 1) * HALF, HEAD_DIM:]
            zero = jnp.zeros_like(gq_b)
            add0 = jnp.where(early, gq_b, zero)
            add1 = gq_a + jnp.where(early, zero, gq_b)
            if first:
                gq_acc[g, :HALF, cols] = add0
                gq_acc[g, HALF:, cols] = add1
            else:
                gq_acc[g, :HALF, cols] += add0
                gq_acc[g, HALF:, cols] += add1
        for t, (xa, ya, xb, yb) in enumerate(((s_a, q_a, s_b, q_b), (p_a, do_a, p_b, do_b))):
            one = dot_nn(over_heads(xa), jnp.concatenate(ya, axis=0))
            second = dot_nn(over_heads(xb), jnp.concatenate(yb, axis=0))
            zero = jnp.zeros_like(second)
            out[g, t, :HALF] = (one + jnp.where(early, second, zero)).astype(BF16)
            out[g, t, HALF:] = jnp.where(early, zero, second).astype(BF16)

    def set_flag(which):
        mine = jnp.max(tile[0])
        flag[which] = (jnp.max(tile[which]) < mine).astype(jnp.int32)

    if COMPUTE:
        own(0)
    for g in range(1, chunks):
        for copy in load_q(g):
            copy.wait()

    def step(t, carry):
        @pl.when(t < chunks)
        def _():
            g = t
            if COMM:
                for x in range(2):
                    hop_pair(g, x).wait_recv()
                    hop_far(g, x).start()

            @pl.when(g + LEAD < chunks)
            def _():
                send_own(g + LEAD, 0)

            if COMM:

                @pl.when(odd == 0)
                def _():
                    hop_up(g).start()

        if COMM:

            @pl.when(t == 0)
            def _():
                tile_pair().wait_recv()
                tile_far().start()

                @pl.when(odd == 0)
                def _():
                    tile_up().start()

            @pl.when(t == 1)
            def _():
                tile_far().wait_recv()

                @pl.when(core == 1)
                def _():
                    tile_near().start()

        @pl.when((t >= 2) & (t < chunks + 2))
        def _():
            g = t - 2
            if COMM:
                for x in range(2):
                    hop_far(g, x).wait_recv()

                @pl.when(core == 1)
                def _():
                    hop_near_far(g).start()

        if COMM:

            @pl.when(t == 3)
            def _():
                @pl.when(odd == 0)
                def _():
                    tile_up().wait_recv()

                tile_near().wait_recv()
                for which in (1, 2, 3):
                    set_flag(which)

        @pl.when((t >= 3) & (t < chunks + 3))
        def _():
            g = t - 3
            if COMM:
                hop_near_own(g).wait_recv()
            if COMPUTE:
                other(g, kv_near, 3, n_send, True)
            if COMM:
                back_near(g).start()
            if COMPUTE:
                other(g, kv_far, 2, f_send, False)
            if COMM:

                @pl.when(core == 0)
                def _():
                    back_far(g).start()

                @pl.when(odd == 0)
                def _():
                    hop_up(g).wait_recv()

            if COMPUTE:
                other(g, kv_grp, 1, g_send, False)
            if COMM:

                @pl.when(odd == 0)
                def _():
                    back_down(g).start()

        if COMM:

            @pl.when((t >= 4) & (t < chunks + 4) & (core == 1))
            def _():
                g = t - 4
                back_near(g).wait_recv()
                f_send[g] = (f_send[g].astype(F32) + n_recv[g].astype(F32)).astype(BF16)
                back_far(g).start()

        if COMPUTE:
            @pl.when(t < 3)
            def _():
                own(t + 1)

            @pl.when((t >= chunks + 3) & (t < 2 * chunks - 1))
            def _():
                own(t + 1 - chunks)

        if COMM:

            @pl.when((t >= 6) & (t < chunks + 6))
            def _():
                g = t - 6
                back_far(g).wait_recv()

                @pl.when(odd == 0)
                def _():
                    back_down(g).wait_recv()
                    s_send[g] = (f_recv[g].astype(F32) + g_recv[g].astype(F32)).astype(BF16)

                @pl.when(odd == 1)
                def _():
                    s_send[g] = (f_recv[g].astype(F32) + g_send[g].astype(F32)).astype(BF16)

                back_sum(g).start()

        @pl.when(t >= 8)
        def _():
            g = t - 8
            gq_out[g] = ((gq_own[g] + gq_acc[g]) * SCALE).astype(BF16)
            store_q(g).start()
            if COMM:
                back_sum(g).wait_recv()
            total = own32[g] + s_recv[g].astype(F32)

            @pl.when(core == 0)
            def _():
                if COMM:
                    back_near(g).wait_recv()
                both = total + n_recv[g].astype(F32)
                own32[g, 0] = both[0] * SCALE
                own32[g, 1] = both[1]

            @pl.when(core == 1)
            def _():
                own32[g, 0] = total[0] * SCALE
                own32[g, 1] = total[1]

            for copy in store_kv(g):
                copy.start()

        return carry

    lax.fori_loop(0, chunks + 8, step, 0)

    def drain(g, carry):
        store_q(g).wait()
        for copy in store_kv(g):
            copy.wait()
        if COMM:
            for x in range(2):
                hop_pair(g, x).wait_send()
                hop_far(g, x).wait_send()
            hop_near_own(g).wait_send()
            back_near(g).wait_send()
            back_far(g).wait_send()
            back_sum(g).wait_send()

            @pl.when(odd == 0)
            def _():
                hop_up(g).wait_send()
                back_down(g).wait_send()

        return carry

    lax.fori_loop(0, chunks, drain, 0)
    if COMM:
        tile_pair().wait_send()
        tile_far().wait_send()
        tile_near().wait_send()

        @pl.when(odd == 0)
        def _():
            tile_up().wait_send()


def on_device(n_outer, n_inner, queries, keys, values, grad_out, log_sum, row_delta, piece_index):
    rows = queries.shape[0]
    chunks = keys.shape[1] // HEAD_DIM
    group = queries.shape[1] // keys.shape[1]
    wide = (chunks, rows, group * HEAD_DIM)
    pair = (chunks, 2, rows, HEAD_DIM)
    hbm = pl.BlockSpec(memory_space=pltpu.HBM)
    vmem = pltpu.VMEM
    return pl.pallas_call(
        functools.partial(kernel, group, n_outer, n_inner),
        out_shape=(
            jax.ShapeDtypeStruct(queries.shape, BF16),
            jax.ShapeDtypeStruct(keys.shape, F32),
            jax.ShapeDtypeStruct(values.shape, F32),
        ),
        in_specs=[hbm] * 6 + [pl.BlockSpec(memory_space=pltpu.SMEM)],
        out_specs=(hbm, hbm, hbm),
        scratch_shapes=[
            vmem(keys.shape, BF16),
            vmem(values.shape, BF16),
            vmem(wide, BF16),
            vmem(wide, BF16),
            vmem(log_sum.shape, F32),
            vmem(row_delta.shape, F32),
            vmem((chunks, group, rows), F32),
            vmem((chunks, group, rows), F32),
            vmem(pair, BF16),
            vmem((2,) + pair, BF16),
            vmem(pair, BF16),
            vmem(pair, BF16),
            vmem(wide, F32),
            vmem(wide, F32),
            vmem(wide, BF16),
            vmem(pair, F32),
            vmem(pair, BF16),
            vmem(pair, BF16),
            vmem(pair, BF16),
            vmem(pair, BF16),
            vmem(pair, BF16),
            vmem(pair, BF16),
            vmem(pair, BF16),
            vmem(pair, BF16),
            vmem((5, 8, 128), F32),
            pltpu.SMEM((4,), jnp.int32),
            pltpu.SemaphoreType.DMA((5, chunks)),
            pltpu.SemaphoreType.DMA((3, chunks)),
            pltpu.SemaphoreType.DMA((2, 4)),
            pltpu.SemaphoreType.DMA((10, chunks)),
            pltpu.SemaphoreType.DMA((10, chunks)),
        ],
        compiler_params=pltpu.CompilerParams(
            collective_id=0 if COMM else None, has_side_effects=True, vmem_limit_bytes=56 * 1024 * 1024
        ),
        cost_estimate=pl.CostEstimate(
            flops=6_000_000_000, bytes_accessed=10_000_000, transcendentals=5_000_000
        ),
    )(queries, keys, values, grad_out, log_sum, row_delta, piece_index)


def solution(mesh):
    in_specs = (
        P(("outer", "inner"), None),
        P(("outer", "inner"), None),
        P(("outer", "inner"), None),
        P(("outer", "inner"), None),
        P(None, ("outer", "inner")),
        P(None, ("outer", "inner")),
        P(("outer", "inner")),
    )
    out_specs = (
        P(("outer", "inner"), None),
        P(("outer", "inner"), None),
        P(("outer", "inner"), None),
    )
    body = functools.partial(on_device, mesh.shape["outer"], mesh.shape["inner"])
    return jax.shard_map(
        body, mesh=mesh, in_specs=in_specs, out_specs=out_specs, check_vma=False
    )
```
